256 devices in a mesh: gx: 16 (over y, x_hi, core), gy: 16 (over z, x_lo).
Axes of the slice: x: 4 (x_hi: 2, x_lo: 2; x = x_hi * 2 + x_lo), y: 4, z: 8, core: 2. Of those that a mesh axis runs over, the one named last changes fastest.
Arguments:
- tokens: bfloat16 [32, 32, 32, 768], P('gx', 'gy'), may hold values from -48 to 48
- w_qkv: bfloat16 [768, 2304], replicated, may hold values from -0.25 to 0.25
- w_out: bfloat16 [768, 768], replicated, may hold values from -0.21875 to 0.21875
- norm_gain: float32 [768], replicated, may hold values from 0.1 to 1.9
- norm_shift: float32 [768], replicated, may hold values from -3 to 3
- w_conv: bfloat16 [3, 3, 3, 768, 256], P(None, None, None, None, 'gx'), may hold values from -0.0390625 to 0.0390625
- conv_bias: float32 [256], replicated, may hold values from -0.5 to 0.5
Outputs:
- decoded: bfloat16 [32, 32, 32, 256], P('gx', 'gy')
The draws below stay inside these ranges and needn't reach their ends.
All inputs are finite; a program needn't handle non-finite values.
Results may differ from the reference program's by a relative error of at most 0.015.
Values may be sent and summed in bfloat16 or wider, within the bound.
No kernel may reach another device: no remote copies, remote signals or barrier semaphores. Data moves between devices by JAX's collectives and lax.ppermute only.
A program may use at most 192 MiB of HBM per device.

```python
import math
import jax
import jax.numpy as jnp
from jax import lax

TZ = 32
D = 768
HEADS = 16
HEAD_DIM = 48
COUT = 256
TX = 32
TY = 32
TOKENS = 32768


def draw_tokens(key, part):
    key = jax.random.fold_in(key, 11)
    first = jax.random.fold_in(key, 0)
    shape = (TX, TY, TZ, D)
    values = jnp.clip(jax.random.normal(first, shape, jnp.float32), -6.0, 6.0)
    return values.astype(jnp.bfloat16)


def block_scale(own_key, extent, shards, smallest, largest):
    def one(axis_at, shards_of):
        draws = jax.random.uniform(jax.random.fold_in(jax.random.fold_in(own_key, 6), axis_at), (shards_of,), jnp.float32, smallest / len(shards), largest / len(shards))
        return jnp.repeat(jnp.exp(draws), extent[axis_at] // shards_of).reshape((-1,) + (1,) * (len(extent) - axis_at - 1))

    level = one(*shards[0])
    for cut in shards[1:]:
        level = level * one(*cut)
    return level


def scatter_about(key, shape, width, reach, cuts=(), dtype=jnp.bfloat16):
    gain = block_scale(key, shape, cuts, -0.22, 0.18) if cuts else 1.0
    entries = jax.random.normal(key, shape, jnp.float32) * width * gain
    return jnp.minimum(jnp.maximum(entries, -reach), reach).astype(dtype)


def setup_inputs(seed: int = 0) -> dict:
    streams_of = jax.random.split(jax.random.key(seed), 8)
    tokens = draw_tokens(jax.random.fold_in(streams_of[7], 71), 0)
    w_qkv = scatter_about(streams_of[1], (D, 3 * D), 0.045, 0.25)
    w_out = scatter_about(streams_of[2], (D, D), D ** -0.5, 0.21875)
    norm_gain = jnp.clip(1.0 + 0.18 * jax.random.normal(streams_of[3], (D,), jnp.float32), 0.1, 1.9)
    norm_shift = scatter_about(streams_of[4], (D,), 0.5, 3.0, (), jnp.float32)
    w_conv = scatter_about(streams_of[5], (3, 3, 3, D, COUT), (27 * D) ** -0.5, 0.0390625, ((4, 16),))
    conv_bias = jnp.clip(jax.random.uniform(streams_of[6], (COUT,), jnp.float32, -0.5, 0.5), -0.5, 0.5)
    return {"tokens": tokens, "w_qkv": w_qkv, "w_out": w_out, "norm_gain": norm_gain, "norm_shift": norm_shift, "w_conv": w_conv, "conv_bias": conv_bias}


def one_head(operands):
    head_q, head_k, head_v = operands
    block_rows = math.gcd(TOKENS, 2048)
    blocks = head_q.reshape(TOKENS // block_rows, block_rows, HEAD_DIM)
    keys_wide = head_k.astype(jnp.float32)
    values_wide = head_v.astype(jnp.float32)

    def per_block(query_block):
        scores = jnp.dot(query_block.astype(jnp.float32), keys_wide.T) / math.sqrt(HEAD_DIM)
        expons = jnp.exp(scores - lax.optimization_barrier(jnp.max(scores, axis=-1, keepdims=True)))
        weights = expons.astype(jnp.bfloat16)
        summed = jnp.dot(weights.astype(jnp.float32), values_wide)
        return (summed / lax.optimization_barrier(jnp.sum(expons, axis=-1, keepdims=True))).astype(jnp.bfloat16)
    return lax.map(per_block, blocks).reshape(TOKENS, HEAD_DIM)

def reference(tokens, w_qkv, w_out, norm_gain, norm_shift, w_conv, conv_bias):
    rows = tokens.reshape(TOKENS, D)
    packed = jnp.dot(rows, w_qkv, preferred_element_type=jnp.float32).astype(jnp.bfloat16)
    query = packed[:, :D].reshape(TOKENS, HEADS, HEAD_DIM).transpose(1, 0, 2)
    keys = packed[:, D:2 * D].reshape(TOKENS, HEADS, HEAD_DIM).transpose(1, 0, 2)
    values = packed[:, 2 * D:].reshape(TOKENS, HEADS, HEAD_DIM).transpose(1, 0, 2)
    attended = lax.map(one_head, (query, keys, values))
    attended = attended.transpose(1, 0, 2).reshape(TOKENS, D)
    projected = jnp.dot(attended, w_out, preferred_element_type=jnp.float32)
    center = lax.optimization_barrier(jnp.mean(projected, axis=-1, keepdims=True))
    spread = lax.optimization_barrier(jnp.mean((projected - center) ** 2, axis=-1, keepdims=True))
    normed = ((projected - center) / jnp.sqrt(spread + 1e-05) * norm_gain + norm_shift).astype(jnp.bfloat16)
    normed = normed.reshape(TX, TY, TZ, D)
    padded = jnp.pad(normed, ((1, 1), (1, 1), (1, 1), (0, 0)), mode='wrap')
    total = jnp.zeros((TOKENS, COUT), jnp.float32)
    for shift_x in range(3):
        for shift_y in range(3):
            for shift_z in range(3):
                window = padded[shift_x:shift_x + TX, shift_y:shift_y + TY, shift_z:shift_z + TZ].reshape(TOKENS, D)
                total = total + jnp.dot(window, w_conv[shift_x, shift_y, shift_z], preferred_element_type=jnp.float32)
    return (total + conv_bias).astype(jnp.bfloat16).reshape(TX, TY, TZ, COUT)
```

```python
import functools
import math

import jax
import jax.numpy as jnp
from jax import lax
from jax.experimental import pallas as pl
from jax.experimental.pallas import tpu as pltpu
from jax.sharding import PartitionSpec as P

HEADS = 16
HD = 48
D = 768
COUT = 256
SRC = 16
T = 128
NQ = SRC * T
CK = SRC * T
Q2 = 2 * NQ
QT = 1024
KROWS = 128
ORS = 64
SHIFT_ROW = 2 * HD
SUM_ROW = HD
SCALE = math.log2(math.e) / math.sqrt(HD)
SAFE_SUM = 2.0**100
VMEM = pl.BlockSpec(memory_space=pltpu.VMEM)
ANY = pl.BlockSpec(memory_space=pl.ANY)
BF = jnp.bfloat16
F32 = jnp.float32


def _params(mb=48):
    return pltpu.CompilerParams(vmem_limit_bytes=mb * 2**20)


def _cost(flops, nbytes, trans=0):
    return pl.CostEstimate(flops=int(flops), bytes_accessed=int(nbytes), transcendentals=int(trans))


def _qkv_kernel(x_ref, w_ref, o_ref):
    x = x_ref[...]
    for part in range(3):
        cols = pl.ds(part * D, D)
        y = jnp.dot(x, w_ref[:, cols], preferred_element_type=F32)
        yt = y.T.astype(BF)
        for h in range(HEADS):
            o_ref[h, part * HD : (part + 1) * HD, :] = yt[h * HD : (h + 1) * HD, :]


def _qkv(x, w):
    return pl.pallas_call(
        _qkv_kernel,
        out_shape=jax.ShapeDtypeStruct((HEADS, 3 * HD, T), BF),
        in_specs=[VMEM, VMEM],
        out_specs=VMEM,
        compiler_params=_params(),
        cost_estimate=_cost(2 * T * D * 3 * D, 5e6),
        name="qkv_projection",
    )(x, w)


def _fill_chunk(kv_ref, kp_ref, vp_ref, base):
    row = lax.broadcasted_iota(jnp.int32, (KROWS - 2 * HD, T), 0)
    shift_on = jnp.where(row < 3, 1.0, 0.0).astype(BF)
    vrow = lax.broadcasted_iota(jnp.int32, (ORS - HD, T), 0)
    ones = jnp.where(vrow == 0, 1.0, 0.0).astype(BF)
    for s in range(SRC):
        kt = kv_ref[s, 0:HD, :]
        block = jnp.concatenate([kt, kt, shift_on], axis=0)
        at = base + s * T
        kp_ref[at : at + T, :] = block.T
        vp_ref[0:HD, at : at + T] = kv_ref[s, HD : 2 * HD, :]
        vp_ref[HD:ORS, at : at + T] = ones


def _set_shift(qa_ref, cols, m):
    hi = m.astype(BF)
    rest = m - hi.astype(F32)
    mid = rest.astype(BF)
    low = (rest - mid.astype(F32)).astype(BF)
    row = lax.broadcasted_iota(jnp.int32, (16, m.shape[1]), 0)
    rows = jnp.where(
        row == 0, hi.astype(F32), jnp.where(row == 1, mid.astype(F32), jnp.where(row == 2, low.astype(F32), 0.0))
    )
    qa_ref[SHIFT_ROW : SHIFT_ROW + 16, cols] = (-rows).astype(BF)


def _tile(i):
    return pl.ds(pl.multiple_of(i * QT, QT), QT)


def _accumulate(qa_ref, kp_ref, vp_ref, acc_in, acc_out, chunks):
    def body(i, carry):
        cols = _tile(i)
        q = qa_ref[:, cols]
        acc = acc_in[:, cols] if acc_in is not None else jnp.zeros((ORS, QT), F32)
        for c in range(chunks):
            s = jnp.dot(kp_ref[c * CK : (c + 1) * CK, :], q, preferred_element_type=F32)
            p = jnp.exp2(s).astype(BF)
            acc = acc + jnp.dot(vp_ref[:, c * CK : (c + 1) * CK], p, preferred_element_type=F32)
        acc_out[:, cols] = acc
        return carry

    lax.fori_loop(0, Q2 // QT, body, 0)


def _first_kernel(q_own, q_sib, kv_ref, qa_ref, m_ref, acc_ref, kp_ref, vp_ref):
    _fill_chunk(kv_ref, kp_ref, vp_ref, 0)
    for part, q_ref in enumerate((q_own, q_sib)):
        for s in range(SRC):
            cols = pl.ds(part * NQ + s * T, T)
            q = q_ref[s, 0:HD, :].astype(F32) * SCALE
            hi = q.astype(BF)
            qa_ref[0:HD, cols] = hi
            qa_ref[HD : 2 * HD, cols] = (q - hi.astype(F32)).astype(BF)
    qa_ref[SHIFT_ROW:KROWS, :] = jnp.zeros((KROWS - SHIFT_ROW, Q2), BF)

    def start(i, carry):
        cols = _tile(i)
        s = jnp.dot(kp_ref[0:256, :], qa_ref[:, cols], preferred_element_type=F32)
        m = jnp.max(s, axis=0, keepdims=True)
        m_ref[:, cols] = jnp.broadcast_to(m, (8, QT))
        _set_shift(qa_ref, cols, m)
        return carry

    lax.fori_loop(0, Q2 // QT, start, 0)
    _accumulate(qa_ref, kp_ref, vp_ref, None, acc_ref, 1)


def _next_kernel(chunks, qa_ref, acc_in, *refs):
    kvs, (acc_out, kp_ref, vp_ref) = refs[:chunks], refs[chunks:]
    for c in range(chunks):
        _fill_chunk(kvs[c], kp_ref, vp_ref, c * CK)
    _accumulate(qa_ref, kp_ref, vp_ref, acc_in, acc_out, chunks)


def _redo(qa_ref, m_ref, acc_ref, kp_ref, vp_ref, kvs, buf, sem):
    def load(c):
        for n, ref in enumerate(kvs):

            @pl.when(c == n)
            def _():
                copy = pltpu.make_async_copy(ref, buf, sem)
                copy.start()
                copy.wait()

        _fill_chunk(buf, kp_ref, vp_ref, 0)

    qa_ref[SHIFT_ROW:KROWS, :] = jnp.zeros((KROWS - SHIFT_ROW, Q2), BF)

    def find(c, carry):
        load(c)

        def body(i, inner):
            cols = _tile(i)
            s = jnp.dot(kp_ref[0:CK, :], qa_ref[:, cols], preferred_element_type=F32)
            m_ref[:, cols] = jnp.maximum(m_ref[:, cols], jnp.max(s, axis=0, keepdims=True))
            return inner

        return lax.fori_loop(0, Q2 // QT, body, carry)

    lax.fori_loop(0, len(kvs), find, 0)

    def shift(i, carry):
        cols = _tile(i)
        _set_shift(qa_ref, cols, m_ref[0:1, cols])
        acc_ref[:, cols] = jnp.zeros((ORS, QT), F32)
        return carry

    lax.fori_loop(0, Q2 // QT, shift, 0)

    def add(c, carry):
        load(c)
        _accumulate(qa_ref, kp_ref, vp_ref, acc_ref, acc_ref, 1)
        return carry

    lax.fori_loop(0, len(kvs), add, 0)


def _last_kernel(qa_in, m_in, acc_in, kv_a, kv_b, *refs):
    kvs, (own_ref, sib_ref, qa_ref, m_ref, acc_ref, kp_ref, vp_ref, buf, sem) = refs[:8], refs[8:]
    half = SRC // 2
    for s in range(half):
        buf[s, :, :] = kv_a[s, :, :]
        buf[half + s, :, :] = kv_b[s, :, :]
    _fill_chunk(buf, kp_ref, vp_ref, 0)
    _accumulate(qa_in, kp_ref, vp_ref, acc_in, acc_ref, 1)
    m_ref[...] = m_in[...]
    good = jnp.max(acc_ref[SUM_ROW : SUM_ROW + 1, :]) < SAFE_SUM

    @pl.when(jnp.logical_not(good))
    def _():
        qa_ref[...] = qa_in[...]
        _redo(qa_ref, m_ref, acc_ref, kp_ref, vp_ref, kvs, buf, sem)

    own_ref[0:56, :] = acc_ref[0:56, 0:NQ]
    own_ref[56:64, :] = m_ref[:, 0:NQ]
    sib_ref[0:56, :] = acc_ref[0:56, NQ:Q2]
    sib_ref[56:64, :] = m_ref[:, NQ:Q2]


def _pair_cost(chunks):
    return _cost(2 * Q2 * CK * 512 * chunks, 4e6, Q2 * CK * chunks)


def _scratch(chunks):
    return [pltpu.VMEM((chunks * CK, KROWS), BF), pltpu.VMEM((ORS, chunks * CK), BF)]


def _first(q_own, q_sib, kv):
    return pl.pallas_call(
        _first_kernel,
        out_shape=(
            jax.ShapeDtypeStruct((KROWS, Q2), BF),
            jax.ShapeDtypeStruct((8, Q2), F32),
            jax.ShapeDtypeStruct((ORS, Q2), F32),
        ),
        in_specs=[VMEM] * 3,
        out_specs=(VMEM,) * 3,
        scratch_shapes=_scratch(1),
        compiler_params=_params(),
        cost_estimate=_pair_cost(1),
        name="attend_own",
    )(q_own, q_sib, kv)


def _next(qa, acc, *kvs):
    n = len(kvs)
    return pl.pallas_call(
        functools.partial(_next_kernel, n),
        out_shape=jax.ShapeDtypeStruct((ORS, Q2), F32),
        in_specs=[VMEM] * (2 + n),
        out_specs=VMEM,
        scratch_shapes=_scratch(n),
        compiler_params=_params(),
        cost_estimate=_pair_cost(n),
        name="attend_ring",
    )(qa, acc, *kvs)


def _last(qa, m, acc, kv_a, kv_b, kvs):
    return pl.pallas_call(
        _last_kernel,
        out_shape=(jax.ShapeDtypeStruct((64, NQ), F32), jax.ShapeDtypeStruct((64, NQ), F32)),
        in_specs=[VMEM] * 5 + [ANY] * 8,
        out_specs=(VMEM, VMEM),
        scratch_shapes=[
            pltpu.VMEM((KROWS, Q2), BF),
            pltpu.VMEM((8, Q2), F32),
            pltpu.VMEM((ORS, Q2), F32),
            *_scratch(1),
            pltpu.VMEM((SRC, 2 * HD, T), BF),
            pltpu.SemaphoreType.DMA,
        ],
        compiler_params=_params(),
        cost_estimate=_pair_cost(1),
        name="attend_last",
    )(qa, m, acc, kv_a, kv_b, *kvs)


def _merge_kernel(a_ref, b_ref, o_ref):
    ma, mb = a_ref[56:57, :], b_ref[56:57, :]
    top = jnp.maximum(ma, mb)
    wa, wb = jnp.exp2(ma - top), jnp.exp2(mb - top)
    total = a_ref[SUM_ROW : SUM_ROW + 1, :] * wa + b_ref[SUM_ROW : SUM_ROW + 1, :] * wb
    out = ((a_ref[0:HD, :] * wa + b_ref[0:HD, :] * wb) / total).astype(BF)
    for s in range(SRC):
        o_ref[s, :, :] = out[:, s * T : (s + 1) * T]


def _merge(a, b):
    return pl.pallas_call(
        _merge_kernel,
        out_shape=jax.ShapeDtypeStruct((SRC, HD, T), BF),
        in_specs=[VMEM, VMEM],
        out_specs=VMEM,
        compiler_params=_params(),
        cost_estimate=_cost(1e6, 2e6),
        name="merge_cores",
    )(a, b)


def _norm_kernel(att_ref, w_ref, gain_ref, shift_ref, o_ref):
    att = att_ref[...].astype(F32).T.astype(BF)
    y = jnp.dot(att, w_ref[...], preferred_element_type=F32)
    center = jnp.mean(y, axis=-1, keepdims=True)
    spread = jnp.mean((y - center) ** 2, axis=-1, keepdims=True)
    o_ref[...] = ((y - center) / jnp.sqrt(spread + 1e-05) * gain_ref[...] + shift_ref[...]).astype(BF)


def _norm(att, w, gain, shift):
    return pl.pallas_call(
        _norm_kernel,
        out_shape=jax.ShapeDtypeStruct((T, D), BF),
        in_specs=[VMEM] * 4,
        out_specs=VMEM,
        compiler_params=_params(),
        cost_estimate=_cost(2 * T * D * D, 2e6),
        name="project_norm",
    )(att, w, gain.reshape(1, D), shift.reshape(1, D))


def _conv_kernel(x_ref, w_ref, b_ref, o_ref, acc_ref):
    step = pl.program_id(0)
    a, b = step // 3, step % 3
    window = x_ref[pl.ds(a, 2), pl.ds(b, 2)].reshape(T, D)
    y = lax.dot_general(
        window, w_ref[...].reshape(3 * COUT, D), (((1,), (1,)), ((), ())), preferred_element_type=F32
    )

    @pl.when(step == 0)
    def _():
        acc_ref[...] = y

    @pl.when(step > 0)
    def _():
        acc_ref[...] += y

    @pl.when(step == 8)
    def _():
        for col in range(4):
            rows = slice(col * 32, (col + 1) * 32)
            first = acc_ref[rows, 0:COUT]
            mid = acc_ref[rows, COUT : 2 * COUT]
            last = acc_ref[rows, 2 * COUT : 3 * COUT]
            first = jnp.concatenate([first[31:32], first[0:31]], axis=0)
            last = jnp.concatenate([last[1:32], last[0:1]], axis=0)
            o_ref[rows, :] = (first + mid + last + b_ref[...]).astype(BF)


def _conv(padded, w, bias):
    return pl.pallas_call(
        _conv_kernel,
        out_shape=jax.ShapeDtypeStruct((T, COUT), BF),
        grid=(9,),
        in_specs=[
            pl.BlockSpec((4, 4, 32, D), lambda i: (0, 0, 0, 0)),
            pl.BlockSpec((3, COUT, D), lambda i: (i, 0, 0)),
            pl.BlockSpec((1, COUT), lambda i: (0, 0)),
        ],
        out_specs=pl.BlockSpec((T, COUT), lambda i: (0, 0)),
        scratch_shapes=[pltpu.VMEM((T, 3 * COUT), F32)],
        compiler_params=_params(),
        cost_estimate=_cost(2 * T * D * COUT * 27, 12e6),
        name="convolution",
    )(padded, w, bias.reshape(1, COUT))


def _linear(y, xh, c, z, xl):
    return (y * 4 + xh * 2 + c) * 16 + z * 2 + xl


PLANES = [
    [_linear(y, xh, c, z, xl) for y in range(4) for xh in range(2) for xl in range(2)]
    for z in range(8)
    for c in range(2)
]


def _plane_swap(x):
    return lax.all_to_all(x, ("gx", "gy"), split_axis=0, concat_axis=0, tiled=True, axis_index_groups=PLANES)


def _core_swap(x):
    return lax.ppermute(x, "gx", [(i, i ^ 1) for i in range(16)])


def _along_z(x, d):
    return lax.ppermute(x, "gy", [(z * 2 + l, ((z + d) % 8) * 2 + l) for z in range(8) for l in range(2)])


def _halo(block):
    up = [(i, (i + 1) % 16) for i in range(16)]
    down = [(i, (i - 1) % 16) for i in range(16)]
    for axis, dim in (("gx", 0), ("gy", 1)):
        size = block.shape[dim]
        low = lax.ppermute(lax.slice_in_dim(block, size - 1, size, axis=dim), axis, up)
        high = lax.ppermute(lax.slice_in_dim(block, 0, 1, axis=dim), axis, down)
        block = jnp.concatenate([low, block, high], axis=dim)
    return block


def shards(tokens, w_qkv, w_out, norm_gain, norm_shift, w_conv, conv_bias):
    packed = _qkv(tokens.reshape(T, D), w_qkv)
    mine = _plane_swap(packed)
    w_taps = jnp.transpose(w_conv, (0, 1, 2, 4, 3)).reshape(27, COUT // 16, D)
    mine, w_taps = lax.optimization_barrier((mine, w_taps))
    taps = lax.all_gather(w_taps, "gx", axis=1, tiled=True)
    q_own, kv = mine[:, :HD], mine[:, HD:]
    up, down = _along_z(kv, 1), _along_z(kv, -1)
    q_sib = _core_swap(q_own)
    qa, m, acc = _first(q_own, q_sib, kv)
    chunks = [kv, up, down]
    for _ in range(2):
        later = (_along_z(up, 1), _along_z(down, -1))
        acc = _next(qa, acc, up, down)
        up, down = later
        chunks += [up, down]
    half = SRC // 2
    far = (_along_z(up[:half], 1), _along_z(down[half:], -1))
    acc = _next(qa, acc, up, down)
    own, sib = _last(qa, m, acc, far[0], far[1], chunks + [jnp.concatenate(far, axis=0)])
    att = _merge(own, _core_swap(sib))
    back = _plane_swap(att).reshape(D, T)
    normed = _norm(back, w_out, norm_gain, norm_shift)
    padded = _halo(normed.reshape(2, 2, 32, D))
    return _conv(padded, taps, conv_bias).reshape(2, 2, 32, COUT)


def solution(mesh):
    return jax.shard_map(
        shards,
        mesh=mesh,
        in_specs=(
            P("gx", "gy", None, None),
            P(),
            P(),
            P(),
            P(),
            P(None, None, None, None, "gx"),
            P(),
        ),
        out_specs=P("gx", "gy", None, None),
        check_vma=False,
    )
```

```python
import functools
import math

import jax
import jax.numpy as jnp
from jax import lax
from jax.experimental import pallas as pl
from jax.experimental.pallas import tpu as pltpu
from jax.sharding import PartitionSpec as P

HEADS = 16
HD = 48
D = 768
COUT = 256
SRC = 16
T = 128
NQ = SRC * T
CK = SRC * T
Q2 = 2 * NQ
QT = 1024
QKV_CUTS = 3
QB, NT, KT = 2048, 512, 256
KROWS = 128
ORS = 64
SHIFT_ROW = 2 * HD
SUM_ROW = HD
M_ROW = 56
SCALE = math.log2(math.e) / math.sqrt(HD)
SAFE_SUM = 2.0**100
VMEM = pl.BlockSpec(memory_space=pltpu.VMEM)
ANY = pl.BlockSpec(memory_space=pl.ANY)
BF = jnp.bfloat16
F32 = jnp.float32


def _params(mb=32):
    return pltpu.CompilerParams(vmem_limit_bytes=mb * 2**20)


def _cost(flops, nbytes, trans=0):
    return pl.CostEstimate(flops=int(flops), bytes_accessed=int(nbytes), transcendentals=int(trans))


def _qkv_kernel(x_hbm, w_hbm, o_ref, x_ref, w_ref, acc_ref, sems):
    copies = [pltpu.make_async_copy(x_hbm, x_ref, sems.at[0])]
    rows = D // QKV_CUTS
    for n in range(QKV_CUTS):
        part = pl.ds(n * rows, rows)
        copies.append(pltpu.make_async_copy(w_hbm.at[part], w_ref.at[part], sems.at[n + 1]))
    for copy in copies:
        copy.start()
    copies[0].wait()
    for n in range(QKV_CUTS):
        copies[n + 1].wait()
        part = slice(n * rows, (n + 1) * rows)
        y = jnp.dot(x_ref[:, part], w_ref[part, :], preferred_element_type=F32)
        acc_ref[...] = y if n == 0 else acc_ref[...] + y
    for part in range(3):
        yt = acc_ref[:, part * D : (part + 1) * D].T.astype(BF)
        for h in range(HEADS):
            o_ref[h, part * HD : (part + 1) * HD, :] = yt[h * HD : (h + 1) * HD, :]


def _qkv(x, w):
    return pl.pallas_call(
        _qkv_kernel,
        out_shape=jax.ShapeDtypeStruct((HEADS, 3 * HD, T), BF),
        in_specs=[ANY, ANY],
        out_specs=VMEM,
        scratch_shapes=[
            pltpu.VMEM((T, D), BF),
            pltpu.VMEM((D, 3 * D), BF),
            pltpu.VMEM((T, 3 * D), F32),
            pltpu.SemaphoreType.DMA((QKV_CUTS + 1,)),
        ],
        compiler_params=_params(58),
        cost_estimate=_cost(2 * T * D * 3 * D, 5e6),
        name="qkv_projection",
    )(x, w)


def _fill_chunk(kv_ref, kp_ref, vp_ref, base):
    row = lax.broadcasted_iota(jnp.int32, (KROWS - 2 * HD, T), 0)
    shift_on = jnp.where(row < 3, 1.0, 0.0).astype(BF)
    vrow = lax.broadcasted_iota(jnp.int32, (ORS - HD, T), 0)
    ones = jnp.where(vrow == 0, 1.0, 0.0).astype(BF)
    for s in range(SRC):
        kt = kv_ref[s, 0:HD, :]
        block = jnp.concatenate([kt, kt, shift_on], axis=0)
        at = base + s * T
        kp_ref[at : at + T, :] = block.T
        vp_ref[0:HD, at : at + T] = kv_ref[s, HD : 2 * HD, :]
        vp_ref[HD:ORS, at : at + T] = ones


def _set_shift(qa_ref, cols, m):
    hi = m.astype(BF)
    rest = m - hi.astype(F32)
    mid = rest.astype(BF)
    low = (rest - mid.astype(F32)).astype(BF)
    row = lax.broadcasted_iota(jnp.int32, (16, m.shape[1]), 0)
    rows = jnp.where(
        row == 0, hi.astype(F32), jnp.where(row == 1, mid.astype(F32), jnp.where(row == 2, low.astype(F32), 0.0))
    )
    qa_ref[SHIFT_ROW : SHIFT_ROW + 16, cols] = (-rows).astype(BF)


def _tile(i):
    return pl.ds(pl.multiple_of(i * QT, QT), QT)


def _accumulate(qa_ref, kp_ref, vp_ref, acc_in, acc_out, chunks):
    keys, tiles = chunks * CK // KT, QB // NT

    def body(i, carry):
        def cols(t):
            return pl.ds(pl.multiple_of(i * QB + t * NT, NT), NT)

        q = [qa_ref[:, cols(t)] for t in range(tiles)]
        acc = [acc_in[:, cols(t)] if acc_in is not None else jnp.zeros((ORS, NT), F32) for t in range(tiles)]
        steps = [(k, t) for k in range(keys) for t in range(tiles)]
        scores, weights = {}, {}
        for n in range(len(steps) + 2):
            if n < len(steps):
                k, t = steps[n]
                scores[n] = jnp.dot(kp_ref[k * KT : (k + 1) * KT, :], q[t], preferred_element_type=F32)
            if 0 <= n - 1 < len(steps):
                weights[n - 1] = jnp.exp2(scores.pop(n - 1)).astype(BF)
            if 0 <= n - 2:
                k, t = steps[n - 2]
                acc[t] = acc[t] + jnp.dot(
                    vp_ref[:, k * KT : (k + 1) * KT], weights.pop(n - 2), preferred_element_type=F32
                )
        for t in range(tiles):
            acc_out[:, cols(t)] = acc[t]
        return carry

    lax.fori_loop(0, Q2 // QB, body, 0)


def _first_kernel(q_own, q_sib, kv_ref, qa_ref, m_ref, acc_ref, kp_ref, vp_ref):
    _fill_chunk(kv_ref, kp_ref, vp_ref, 0)
    for part, q_ref in enumerate((q_own, q_sib)):
        for s in range(SRC):
            cols = pl.ds(part * NQ + s * T, T)
            q = q_ref[s, 0:HD, :].astype(F32) * SCALE
            hi = q.astype(BF)
            qa_ref[0:HD, cols] = hi
            qa_ref[HD : 2 * HD, cols] = (q - hi.astype(F32)).astype(BF)
    qa_ref[SHIFT_ROW:KROWS, :] = jnp.zeros((KROWS - SHIFT_ROW, Q2), BF)

    def start(i, carry):
        cols = _tile(i)
        s = jnp.dot(kp_ref[0:256, :], qa_ref[:, cols], preferred_element_type=F32)
        m = jnp.max(s, axis=0, keepdims=True)
        m_ref[:, cols] = jnp.broadcast_to(m, (8, QT))
        _set_shift(qa_ref, cols, m)
        return carry

    lax.fori_loop(0, Q2 // QT, start, 0)
    _accumulate(qa_ref, kp_ref, vp_ref, None, acc_ref, 1)


def _next_kernel(chunks, qa_ref, acc_in, *refs):
    kvs, (acc_out, kp_ref, vp_ref) = refs[:chunks], refs[chunks:]
    for c in range(chunks):
        _fill_chunk(kvs[c], kp_ref, vp_ref, c * CK)
    _accumulate(qa_ref, kp_ref, vp_ref, acc_in, acc_out, chunks)


def _redo(qa_ref, m_ref, acc_ref, kp_ref, vp_ref, kvs, kv_a, kv_b, buf, sem):
    def load(c):
        for n, ref in enumerate(kvs):

            @pl.when(c == n)
            def _():
                copy = pltpu.make_async_copy(ref, buf, sem)
                copy.start()
                copy.wait()

        @pl.when(c == len(kvs))
        def _():
            buf[0 : SRC // 2] = kv_a[...]
            buf[SRC // 2 : SRC] = kv_b[...]

        _fill_chunk(buf, kp_ref, vp_ref, 0)

    qa_ref[SHIFT_ROW:KROWS, :] = jnp.zeros((KROWS - SHIFT_ROW, Q2), BF)

    def find(c, carry):
        load(c)

        def body(i, inner):
            cols = _tile(i)
            s = jnp.dot(kp_ref[0:CK, :], qa_ref[:, cols], preferred_element_type=F32)
            m_ref[:, cols] = jnp.maximum(m_ref[:, cols], jnp.max(s, axis=0, keepdims=True))
            return inner

        return lax.fori_loop(0, Q2 // QT, body, carry)

    lax.fori_loop(0, len(kvs) + 1, find, 0)

    def shift(i, carry):
        cols = _tile(i)
        _set_shift(qa_ref, cols, m_ref[0:1, cols])
        acc_ref[:, cols] = jnp.zeros((ORS, QT), F32)
        return carry

    lax.fori_loop(0, Q2 // QT, shift, 0)

    def add(c, carry):
        load(c)
        _accumulate(qa_ref, kp_ref, vp_ref, acc_ref, acc_ref, 1)
        return carry

    lax.fori_loop(0, len(kvs) + 1, add, 0)


def _last_kernel(qa_in, m_in, acc_in, kv_a, kv_b, *refs):
    kvs, (out_ref, qa_ref, m_ref, kp_ref, vp_ref, buf, sem) = refs[:7], refs[7:]
    half = SRC // 2
    for s in range(half):
        buf[s, :, :] = kv_a[s, :, :]
        buf[half + s, :, :] = kv_b[s, :, :]
    _fill_chunk(buf, kp_ref, vp_ref, 0)
    _accumulate(qa_in, kp_ref, vp_ref, acc_in, out_ref, 1)
    m_ref[...] = m_in[...]
    good = jnp.max(out_ref[SUM_ROW : SUM_ROW + 1, :]) < SAFE_SUM

    @pl.when(jnp.logical_not(good))
    def _():
        qa_ref[...] = qa_in[...]
        _redo(qa_ref, m_ref, out_ref, kp_ref, vp_ref, kvs, kv_a, kv_b, buf, sem)

    out_ref[M_ROW:ORS, :] = m_ref[...]


def _pair_cost(chunks):
    return _cost(2 * Q2 * CK * 512 * chunks, 4e6, Q2 * CK * chunks)


def _scratch(chunks):
    return [pltpu.VMEM((chunks * CK, KROWS), BF), pltpu.VMEM((ORS, chunks * CK), BF)]


def _first(q_own, q_sib, kv):
    return pl.pallas_call(
        _first_kernel,
        out_shape=(
            jax.ShapeDtypeStruct((KROWS, Q2), BF),
            jax.ShapeDtypeStruct((8, Q2), F32),
            jax.ShapeDtypeStruct((ORS, Q2), F32),
        ),
        in_specs=[VMEM] * 3,
        out_specs=(VMEM,) * 3,
        scratch_shapes=_scratch(1),
        compiler_params=_params(),
        cost_estimate=_pair_cost(1),
        name="attend_own",
    )(q_own, q_sib, kv)


def _next(qa, acc, *kvs):
    n = len(kvs)
    return pl.pallas_call(
        functools.partial(_next_kernel, n),
        out_shape=jax.ShapeDtypeStruct((ORS, Q2), F32),
        in_specs=[VMEM] * (2 + n),
        out_specs=VMEM,
        scratch_shapes=_scratch(n),
        compiler_params=_params(),
        cost_estimate=_pair_cost(n),
        name="attend_ring",
    )(qa, acc, *kvs)


def _last(qa, m, acc, kv_a, kv_b, kvs):
    return pl.pallas_call(
        _last_kernel,
        out_shape=jax.ShapeDtypeStruct((ORS, Q2), F32),
        in_specs=[VMEM] * 5 + [ANY] * 7,
        out_specs=VMEM,
        scratch_shapes=[
            pltpu.VMEM((KROWS, Q2), BF),
            pltpu.VMEM((8, Q2), F32),
            *_scratch(1),
            pltpu.VMEM((SRC, 2 * HD, T), BF),
            pltpu.SemaphoreType.DMA,
        ],
        compiler_params=_params(),
        cost_estimate=_pair_cost(1),
        name="attend_last",
    )(qa, m, acc, kv_a, kv_b, *kvs)


def _merge_kernel(a_ref, b_ref, o_ref, own_ref, sib_ref):
    c = lax.rem(lax.axis_index("gx"), 2)
    for dst, mine, other in ((own_ref, 0, NQ), (sib_ref, NQ, 0)):
        a, b = slice(mine, mine + NQ), slice(other, other + NQ)
        ma, mb = a_ref[M_ROW : M_ROW + 1, a], b_ref[M_ROW : M_ROW + 1, b]
        top = jnp.maximum(ma, mb)
        wa, wb = jnp.exp2(ma - top), jnp.exp2(mb - top)
        total = a_ref[SUM_ROW : SUM_ROW + 1, a] * wa + b_ref[SUM_ROW : SUM_ROW + 1, b] * wb
        out = (a_ref[0:HD, a] * wa + b_ref[0:HD, b] * wb) / total
        for s in range(SRC):
            dst[s, :, :] = out[:, s * T : (s + 1) * T]
    lane = lax.broadcasted_iota(jnp.int32, (HD, T), 1)
    first = lane < 64
    y = lax.rem(lax.div(lane, 32), 2)
    for k in range(8):
        after, before = lax.rem(k + c, 8), lax.rem(k + 7 + c, 8)
        for xl in range(2):
            s = k * 2 + xl
            o_ref[s, :, 0:T] = own_ref[s].astype(BF)
            sides = jnp.where(first, sib_ref[after * 2 + xl], sib_ref[before * 2 + xl])
            o_ref[s, :, T : 2 * T] = sides.astype(BF)
            corners = jnp.where(first, sib_ref[after * 2 + 1 - xl], sib_ref[before * 2 + 1 - xl])
            corners = pltpu.roll(corners, 32 if xl == 0 else T - 32, 1)
            o_ref[s, :, 2 * T : 3 * T] = jnp.where(y == xl, own_ref[k * 2 + 1 - xl], corners).astype(BF)


def _merge(a, b):
    return pl.pallas_call(
        _merge_kernel,
        out_shape=jax.ShapeDtypeStruct((SRC, HD, 3 * T), BF),
        in_specs=[VMEM, VMEM],
        out_specs=VMEM,
        scratch_shapes=[pltpu.VMEM((SRC, HD, T), F32)] * 2,
        compiler_params=_params(16),
        cost_estimate=_cost(1e6, 3e6),
        name="merge_cores",
    )(a, b)


def _norm_kernel(att_ref, w_ref, gain_ref, shift_ref, body_ref, edge_ref):
    xl = lax.rem(lax.axis_index("gy"), 2)
    for part in range(3):
        att = att_ref[:, part * T : (part + 1) * T].astype(F32).T.astype(BF)
        v = jnp.dot(att, w_ref[...], preferred_element_type=F32)
        center = jnp.mean(v, axis=-1, keepdims=True)
        spread = jnp.mean((v - center) ** 2, axis=-1, keepdims=True)
        n = ((v - center) / jnp.sqrt(spread + 1e-05) * gain_ref[...] + shift_ref[...]).astype(BF)
        for x in range(2):
            for y in range(2):
                rows = n[(x * 2 + y) * 32 : (x * 2 + y + 1) * 32]
                side = 3 - 3 * x
                layer = y + xl * (1 - 2 * y)
                if part == 0:
                    body_ref[layer, 1 + x] = rows
                elif part == 1:
                    body_ref[layer, side] = rows
                else:
                    inner = xl if y == 1 else 1 - xl
                    body_ref[2, inner * (1 + x) + (1 - inner) * side] = rows
    edge_ref[...] = body_ref[0]


def _norm(att, w, gain, shift):
    return pl.pallas_call(
        _norm_kernel,
        out_shape=(jax.ShapeDtypeStruct((3, 4, 32, D), BF), jax.ShapeDtypeStruct((4, 32, D), BF)),
        in_specs=[VMEM] * 4,
        out_specs=(VMEM, VMEM),
        compiler_params=_params(16),
        cost_estimate=_cost(6 * T * D * D, 3e6),
        name="project_norm",
    )(att, w, gain.reshape(1, D), shift.reshape(1, D))


def _taps(w_ref, a, layer, xl):
    b = layer + xl * (2 - 2 * layer)
    return w_ref[pl.ds((a * 3 + b) * 3, 3)].reshape(3 * COUT, D)


def _product(w, window):
    return lax.dot_general(
        w, window.reshape(T, D), (((1,), (1,)), ((), ())), preferred_element_type=F32
    )


def _conv_inner_kernel(body_ref, w_ref, acc_ref):
    xl = lax.rem(lax.axis_index("gy"), 2)
    total = None
    for a in range(3):
        for layer in (1, 2):
            y = _product(_taps(w_ref, a, layer, xl), body_ref[layer - 1 : layer + 1, a : a + 2])
            total = y if total is None else total + y
    acc_ref[...] = total


def _conv_outer_kernel(outer_ref, edge_ref, w_ref, acc_ref, b_ref, o_ref):
    xl = lax.rem(lax.axis_index("gy"), 2)
    total = acc_ref[...]
    for a in range(3):
        window = jnp.concatenate([outer_ref[a : a + 2], edge_ref[a : a + 2]], axis=0)
        total = total + _product(_taps(w_ref, a, 0, xl), window)
    total = total.T
    for layer in range(2):
        y = layer + xl * (1 - 2 * layer)
        for x in range(2):
            at = (layer * 2 + x) * 32
            rows = slice(at, at + 32)
            first = total[rows, 0:COUT]
            mid = total[rows, COUT : 2 * COUT]
            last = total[rows, 2 * COUT : 3 * COUT]
            first = jnp.concatenate([first[31:32], first[0:31]], axis=0)
            last = jnp.concatenate([last[1:32], last[0:1]], axis=0)
            o_ref[x, y] = (first + mid + last + b_ref[...]).astype(BF)


def _conv_inner(body, w):
    return pl.pallas_call(
        _conv_inner_kernel,
        out_shape=jax.ShapeDtypeStruct((3 * COUT, T), F32),
        in_specs=[VMEM, VMEM],
        out_specs=VMEM,
        compiler_params=_params(24),
        cost_estimate=_cost(2 * T * D * COUT * 18, 12e6),
        name="convolution_inner",
    )(body, w)


def _conv_outer(outer, edge, w, acc, bias):
    return pl.pallas_call(
        _conv_outer_kernel,
        out_shape=jax.ShapeDtypeStruct((2, 2, 32, COUT), BF),
        in_specs=[VMEM] * 5,
        out_specs=VMEM,
        compiler_params=_params(24),
        cost_estimate=_cost(2 * T * D * COUT * 9, 6e6),
        name="convolution_outer",
    )(outer, edge, w, acc, bias.reshape(1, COUT))


def _linear(y, xh, c, z, xl):
    return (y * 4 + xh * 2 + c) * 16 + z * 2 + xl


PLANES = [
    [_linear(y, xh, c, z, xl) for y in range(4) for xh in range(2) for xl in range(2)]
    for z in range(8)
    for c in range(2)
]


def _plane_swap(x):
    return lax.all_to_all(x, ("gx", "gy"), split_axis=0, concat_axis=0, tiled=True, axis_index_groups=PLANES)


def _core_swap(x):
    return lax.ppermute(x, "gx", [(i, i ^ 1) for i in range(16)])


def _along_z(x, d):
    return lax.ppermute(x, "gy", [(z * 2 + l, ((z + d) % 8) * 2 + l) for z in range(8) for l in range(2)])


def _across_z(x):
    return lax.ppermute(x, "gy", [(i, (i + 1 if i % 2 else i - 1) % 16) for i in range(16)])


def shards(tokens, w_qkv, w_out, norm_gain, norm_shift, w_conv, conv_bias):
    packed = _qkv(tokens.reshape(T, D), w_qkv)
    mine = _plane_swap(packed)
    w_taps = jnp.transpose(w_conv, (0, 1, 2, 4, 3)).reshape(27, COUT // 16, D)
    taps = lax.all_gather(w_taps, "gx", axis=1, tiled=True)
    q_own, kv = mine[:, :HD], mine[:, HD:]
    up, down = _along_z(kv, 1), _along_z(kv, -1)
    q_sib = _core_swap(q_own)
    qa, m, acc = _first(q_own, q_sib, kv)
    chunks = [kv, up, down]
    for _ in range(2):
        later = (_along_z(up, 1), _along_z(down, -1))
        acc = _next(qa, acc, up, down)
        up, down = later
        chunks += [up, down]
    half = SRC // 2
    far = (_along_z(up[:half], 1), _along_z(down[half:], -1))
    acc = _next(qa, acc, up, down)
    acc = _last(qa, m, acc, far[0], far[1], chunks)
    att = _merge(acc, _core_swap(acc))
    att, taps = lax.optimization_barrier((att, taps))
    back = _plane_swap(att).reshape(D, 3 * T)
    body, edge = _norm(back, w_out, norm_gain, norm_shift)
    outer = _across_z(edge)
    inner = _conv_inner(body, taps)
    return _conv_outer(outer, edge, taps, inner, conv_bias)


def solution(mesh):
    return jax.shard_map(
        shards,
        mesh=mesh,
        in_specs=(
            P("gx", "gy", None, None),
            P(),
            P(),
            P(),
            P(),
            P(None, None, None, None, "gx"),
            P(),
        ),
        out_specs=P("gx", "gy", None, None),
        check_vma=False,
    )
```

```python
import functools
import math

import jax
import jax.numpy as jnp
from jax import lax
from jax.experimental import pallas as pl
from jax.experimental.pallas import tpu as pltpu
from jax.sharding import PartitionSpec as P

HEADS = 16
HD = 48
D = 768
COUT = 256
SRC = 16
T = 128
NQ = SRC * T
CK = SRC * T
Q2 = 2 * NQ
QT = 1024
QKV_CUTS = 3
QB, NT, KT = 2048, 512, 256
KROWS = 128
ORS = 64
SHIFT_ROW = 2 * HD
SUM_ROW = HD
M_ROW = 49
SENT = 56
SCALE = math.log2(math.e) / math.sqrt(HD)
SAFE_SUM = 2.0**100
VMEM = pl.BlockSpec(memory_space=pltpu.VMEM)
ANY = pl.BlockSpec(memory_space=pl.ANY)
BF = jnp.bfloat16
F32 = jnp.float32


def _params(mb=32):
    return pltpu.CompilerParams(vmem_limit_bytes=mb * 2**20)


def _cost(flops, nbytes, trans=0):
    return pl.CostEstimate(flops=int(flops), bytes_accessed=int(nbytes), transcendentals=int(trans))


def _qkv_kernel(x_hbm, w_hbm, o_ref, x_ref, w_ref, acc_ref, sems):
    copies = [pltpu.make_async_copy(x_hbm, x_ref, sems.at[0])]
    rows = D // QKV_CUTS
    for n in range(QKV_CUTS):
        part = pl.ds(n * rows, rows)
        copies.append(pltpu.make_async_copy(w_hbm.at[part], w_ref.at[part], sems.at[n + 1]))
    for copy in copies:
        copy.start()
    copies[0].wait()
    for n in range(QKV_CUTS):
        copies[n + 1].wait()
        part = slice(n * rows, (n + 1) * rows)
        y = jnp.dot(x_ref[:, part], w_ref[part, :], preferred_element_type=F32)
        acc_ref[...] = y if n == 0 else acc_ref[...] + y
    for part in range(3):
        yt = acc_ref[:, part * D : (part + 1) * D].T.astype(BF)
        for h in range(HEADS):
            o_ref[h, part * HD : (part + 1) * HD, :] = yt[h * HD : (h + 1) * HD, :]


def _qkv(x, w):
    return pl.pallas_call(
        _qkv_kernel,
        out_shape=jax.ShapeDtypeStruct((HEADS, 3 * HD, T), BF),
        in_specs=[ANY, ANY],
        out_specs=VMEM,
        scratch_shapes=[
            pltpu.VMEM((T, D), BF),
            pltpu.VMEM((D, 3 * D), BF),
            pltpu.VMEM((T, 3 * D), F32),
            pltpu.SemaphoreType.DMA((QKV_CUTS + 1,)),
        ],
        compiler_params=_params(58),
        cost_estimate=_cost(2 * T * D * 3 * D, 5e6),
        name="qkv_projection",
    )(x, w)


def _fill_chunk(kv_ref, kp_ref, vp_ref, base):
    row = lax.broadcasted_iota(jnp.int32, (KROWS - 2 * HD, T), 0)
    shift_on = jnp.where(row < 3, 1.0, 0.0).astype(BF)
    vrow = lax.broadcasted_iota(jnp.int32, (ORS - HD, T), 0)
    ones = jnp.where(vrow == 0, 1.0, 0.0).astype(BF)
    for s in range(SRC):
        kt = kv_ref[s, 0:HD, :]
        block = jnp.concatenate([kt, kt, shift_on], axis=0)
        at = base + s * T
        kp_ref[at : at + T, :] = block.T
        vp_ref[0:HD, at : at + T] = kv_ref[s, HD : 2 * HD, :]
        vp_ref[HD:ORS, at : at + T] = ones


def _set_shift(qa_ref, cols, m):
    hi = m.astype(BF)
    rest = m - hi.astype(F32)
    mid = rest.astype(BF)
    low = (rest - mid.astype(F32)).astype(BF)
    row = lax.broadcasted_iota(jnp.int32, (16, m.shape[1]), 0)
    rows = jnp.where(
        row == 0, hi.astype(F32), jnp.where(row == 1, mid.astype(F32), jnp.where(row == 2, low.astype(F32), 0.0))
    )
    qa_ref[SHIFT_ROW : SHIFT_ROW + 16, cols] = (-rows).astype(BF)


def _tile(i):
    return pl.ds(pl.multiple_of(i * QT, QT), QT)


def _accumulate(qa_ref, kp_ref, vp_ref, acc_in, acc_out, chunks):
    keys, tiles = chunks * CK // KT, QB // NT

    def body(i, carry):
        def cols(t):
            return pl.ds(pl.multiple_of(i * QB + t * NT, NT), NT)

        q = [qa_ref[:, cols(t)] for t in range(tiles)]
        acc = [acc_in[:, cols(t)] if acc_in is not None else jnp.zeros((ORS, NT), F32) for t in range(tiles)]
        steps = [(k, t) for k in range(keys) for t in range(tiles)]
        scores, weights = {}, {}
        for n in range(len(steps) + 2):
            if n < len(steps):
                k, t = steps[n]
                scores[n] = jnp.dot(kp_ref[k * KT : (k + 1) * KT, :], q[t], preferred_element_type=F32)
            if 0 <= n - 1 < len(steps):
                weights[n - 1] = jnp.exp2(scores.pop(n - 1)).astype(BF)
            if 0 <= n - 2:
                k, t = steps[n - 2]
                acc[t] = acc[t] + jnp.dot(
                    vp_ref[:, k * KT : (k + 1) * KT], weights.pop(n - 2), preferred_element_type=F32
                )
        for t in range(tiles):
            acc_out[:, cols(t)] = acc[t]
        return carry

    lax.fori_loop(0, Q2 // QB, body, 0)


def _first_kernel(q_own, q_sib, kv_ref, qa_ref, m_ref, acc_ref, kp_ref, vp_ref):
    _fill_chunk(kv_ref, kp_ref, vp_ref, 0)
    for part, q_ref in enumerate((q_own, q_sib)):
        for s in range(SRC):
            cols = pl.ds(part * NQ + s * T, T)
            q = q_ref[s, 0:HD, :].astype(F32) * SCALE
            hi = q.astype(BF)
            qa_ref[0:HD, cols] = hi
            qa_ref[HD : 2 * HD, cols] = (q - hi.astype(F32)).astype(BF)
    qa_ref[SHIFT_ROW:KROWS, :] = jnp.zeros((KROWS - SHIFT_ROW, Q2), BF)

    def start(i, carry):
        cols = _tile(i)
        s = jnp.dot(kp_ref[0:256, :], qa_ref[:, cols], preferred_element_type=F32)
        m = jnp.max(s, axis=0, keepdims=True)
        m_ref[:, cols] = jnp.broadcast_to(m, (8, QT))
        _set_shift(qa_ref, cols, m)
        return carry

    lax.fori_loop(0, Q2 // QT, start, 0)
    _accumulate(qa_ref, kp_ref, vp_ref, None, acc_ref, 1)


def _next_kernel(chunks, qa_ref, acc_in, *refs):
    kvs, (acc_out, kp_ref, vp_ref) = refs[:chunks], refs[chunks:]
    for c in range(chunks):
        _fill_chunk(kvs[c], kp_ref, vp_ref, c * CK)
    _accumulate(qa_ref, kp_ref, vp_ref, acc_in, acc_out, chunks)


def _redo(qa_ref, m_ref, acc_ref, kp_ref, vp_ref, kvs, kv_a, kv_b, buf, sem):
    def load(c):
        for n, ref in enumerate(kvs):

            @pl.when(c == n)
            def _():
                copy = pltpu.make_async_copy(ref, buf, sem)
                copy.start()
                copy.wait()

        @pl.when(c == len(kvs))
        def _():
            buf[0 : SRC // 2] = kv_a[...]
            buf[SRC // 2 : SRC] = kv_b[...]

        _fill_chunk(buf, kp_ref, vp_ref, 0)

    qa_ref[SHIFT_ROW:KROWS, :] = jnp.zeros((KROWS - SHIFT_ROW, Q2), BF)

    def find(c, carry):
        load(c)

        def body(i, inner):
            cols = _tile(i)
            s = jnp.dot(kp_ref[0:CK, :], qa_ref[:, cols], preferred_element_type=F32)
            m_ref[:, cols] = jnp.maximum(m_ref[:, cols], jnp.max(s, axis=0, keepdims=True))
            return inner

        return lax.fori_loop(0, Q2 // QT, body, carry)

    lax.fori_loop(0, len(kvs) + 1, find, 0)

    def shift(i, carry):
        cols = _tile(i)
        _set_shift(qa_ref, cols, m_ref[0:1, cols])
        acc_ref[:, cols] = jnp.zeros((ORS, QT), F32)
        return carry

    lax.fori_loop(0, Q2 // QT, shift, 0)

    def add(c, carry):
        load(c)
        _accumulate(qa_ref, kp_ref, vp_ref, acc_ref, acc_ref, 1)
        return carry

    lax.fori_loop(0, len(kvs) + 1, add, 0)


def _last_kernel(qa_in, m_in, acc_in, kv_a, kv_b, *refs):
    kvs, (sent_ref, out_ref, qa_ref, m_ref, kp_ref, vp_ref, buf, sem) = refs[:7], refs[7:]
    half = SRC // 2
    for s in range(half):
        buf[s, :, :] = kv_a[s, :, :]
        buf[half + s, :, :] = kv_b[s, :, :]
    _fill_chunk(buf, kp_ref, vp_ref, 0)
    _accumulate(qa_in, kp_ref, vp_ref, acc_in, out_ref, 1)
    m_ref[...] = m_in[...]
    good = jnp.max(out_ref[SUM_ROW : SUM_ROW + 1, :]) < SAFE_SUM

    @pl.when(jnp.logical_not(good))
    def _():
        qa_ref[...] = qa_in[...]
        _redo(qa_ref, m_ref, out_ref, kp_ref, vp_ref, kvs, kv_a, kv_b, buf, sem)

    sent_ref[0:HD, :] = out_ref[0:HD, :]
    row = lax.broadcasted_iota(jnp.int32, (8, Q2), 0)
    sent_ref[HD:SENT, :] = jnp.where(row == 0, out_ref[HD:SENT, :], m_ref[...])


def _pair_cost(chunks):
    return _cost(2 * Q2 * CK * 512 * chunks, 4e6, Q2 * CK * chunks)


def _scratch(chunks):
    return [pltpu.VMEM((chunks * CK, KROWS), BF), pltpu.VMEM((ORS, chunks * CK), BF)]


def _first(q_own, q_sib, kv):
    return pl.pallas_call(
        _first_kernel,
        out_shape=(
            jax.ShapeDtypeStruct((KROWS, Q2), BF),
            jax.ShapeDtypeStruct((8, Q2), F32),
            jax.ShapeDtypeStruct((ORS, Q2), F32),
        ),
        in_specs=[VMEM] * 3,
        out_specs=(VMEM,) * 3,
        scratch_shapes=_scratch(1),
        compiler_params=_params(),
        cost_estimate=_pair_cost(1),
        name="attend_own",
    )(q_own, q_sib, kv)


def _next(qa, acc, *kvs):
    n = len(kvs)
    return pl.pallas_call(
        functools.partial(_next_kernel, n),
        out_shape=jax.ShapeDtypeStruct((ORS, Q2), F32),
        in_specs=[VMEM] * (2 + n),
        out_specs=VMEM,
        scratch_shapes=_scratch(n),
        compiler_params=_params(),
        cost_estimate=_pair_cost(n),
        name="attend_ring",
    )(qa, acc, *kvs)


def _last(qa, m, acc, kv_a, kv_b, kvs):
    return pl.pallas_call(
        _last_kernel,
        out_shape=jax.ShapeDtypeStruct((SENT, Q2), F32),
        in_specs=[VMEM] * 5 + [ANY] * 7,
        out_specs=VMEM,
        scratch_shapes=[
            pltpu.VMEM((ORS, Q2), F32),
            pltpu.VMEM((KROWS, Q2), BF),
            pltpu.VMEM((8, Q2), F32),
            *_scratch(1),
            pltpu.VMEM((SRC, 2 * HD, T), BF),
            pltpu.SemaphoreType.DMA,
        ],
        compiler_params=_params(),
        cost_estimate=_pair_cost(1),
        name="attend_last",
    )(qa, m, acc, kv_a, kv_b, *kvs)


def _merge_kernel(a_ref, b_ref, o_ref, own_ref, sib_ref):
    c = lax.rem(lax.axis_index("gx"), 2)
    for dst, mine, other in ((own_ref, 0, NQ), (sib_ref, NQ, 0)):
        a, b = slice(mine, mine + NQ), slice(other, other + NQ)
        ma, mb = a_ref[M_ROW : M_ROW + 1, a], b_ref[M_ROW : M_ROW + 1, b]
        top = jnp.maximum(ma, mb)
        wa, wb = jnp.exp2(ma - top), jnp.exp2(mb - top)
        total = a_ref[SUM_ROW : SUM_ROW + 1, a] * wa + b_ref[SUM_ROW : SUM_ROW + 1, b] * wb
        out = (a_ref[0:HD, a] * wa + b_ref[0:HD, b] * wb) / total
        for s in range(SRC):
            dst[s, :, :] = out[:, s * T : (s + 1) * T]
    lane = lax.broadcasted_iota(jnp.int32, (HD, T), 1)
    first = lane < 64
    y = lax.rem(lax.div(lane, 32), 2)
    for k in range(8):
        after, before = lax.rem(k + c, 8), lax.rem(k + 7 + c, 8)
        for xl in range(2):
            s = k * 2 + xl
            o_ref[s, :, 0:T] = own_ref[s].astype(BF)
            sides = jnp.where(first, sib_ref[after * 2 + xl], sib_ref[before * 2 + xl])
            o_ref[s, :, T : 2 * T] = sides.astype(BF)
            corners = jnp.where(first, sib_ref[after * 2 + 1 - xl], sib_ref[before * 2 + 1 - xl])
            corners = pltpu.roll(corners, 32 if xl == 0 else T - 32, 1)
            o_ref[s, :, 2 * T : 3 * T] = jnp.where(y == xl, own_ref[k * 2 + 1 - xl], corners).astype(BF)


def _merge(a, b):
    return pl.pallas_call(
        _merge_kernel,
        out_shape=jax.ShapeDtypeStruct((SRC, HD, 3 * T), BF),
        in_specs=[VMEM, VMEM],
        out_specs=VMEM,
        scratch_shapes=[pltpu.VMEM((SRC, HD, T), F32)] * 2,
        compiler_params=_params(16),
        cost_estimate=_cost(1e6, 3e6),
        name="merge_cores",
    )(a, b)


def _norm_kernel(att_ref, w_ref, gain_ref, shift_ref, body_ref, edge_ref):
    xl = lax.rem(lax.axis_index("gy"), 2)
    for part in range(3):
        att = att_ref[:, part * T : (part + 1) * T].astype(F32).T.astype(BF)
        v = jnp.dot(att, w_ref[...], preferred_element_type=F32)
        center = jnp.mean(v, axis=-1, keepdims=True)
        spread = jnp.mean((v - center) ** 2, axis=-1, keepdims=True)
        n = ((v - center) / jnp.sqrt(spread + 1e-05) * gain_ref[...] + shift_ref[...]).astype(BF)
        for x in range(2):
            for y in range(2):
                rows = n[(x * 2 + y) * 32 : (x * 2 + y + 1) * 32]
                side = 3 - 3 * x
                layer = y + xl * (1 - 2 * y)
                if part == 0:
                    body_ref[layer, 1 + x] = rows
                elif part == 1:
                    body_ref[layer, side] = rows
                else:
                    inner = xl if y == 1 else 1 - xl
                    body_ref[2, inner * (1 + x) + (1 - inner) * side] = rows
    edge_ref[...] = body_ref[0]


def _norm(att, w, gain, shift):
    return pl.pallas_call(
        _norm_kernel,
        out_shape=(jax.ShapeDtypeStruct((3, 4, 32, D), BF), jax.ShapeDtypeStruct((4, 32, D), BF)),
        in_specs=[VMEM] * 4,
        out_specs=(VMEM, VMEM),
        compiler_params=_params(16),
        cost_estimate=_cost(6 * T * D * D, 3e6),
        name="project_norm",
    )(att, w, gain.reshape(1, D), shift.reshape(1, D))


def _taps(w_ref, a, layer, xl):
    b = layer + xl * (2 - 2 * layer)
    return w_ref[pl.ds((a * 3 + b) * 3, 3)].reshape(3 * COUT, D)


def _product(w, window):
    return lax.dot_general(
        w, window.reshape(T, D), (((1,), (1,)), ((), ())), preferred_element_type=F32
    )


def _conv_inner_kernel(body_ref, w_ref, acc_ref):
    xl = lax.rem(lax.axis_index("gy"), 2)
    total = None
    for a in range(3):
        for layer in (1, 2):
            y = _product(_taps(w_ref, a, layer, xl), body_ref[layer - 1 : layer + 1, a : a + 2])
            total = y if total is None else total + y
    acc_ref[...] = total


def _conv_outer_kernel(outer_ref, edge_ref, w_ref, acc_ref, b_ref, o_ref):
    xl = lax.rem(lax.axis_index("gy"), 2)
    total = acc_ref[...]
    for a in range(3):
        window = jnp.concatenate([outer_ref[a : a + 2], edge_ref[a : a + 2]], axis=0)
        total = total + _product(_taps(w_ref, a, 0, xl), window)
    total = total.T
    for layer in range(2):
        y = layer + xl * (1 - 2 * layer)
        for x in range(2):
            at = (layer * 2 + x) * 32
            rows = slice(at, at + 32)
            first = total[rows, 0:COUT]
            mid = total[rows, COUT : 2 * COUT]
            last = total[rows, 2 * COUT : 3 * COUT]
            first = jnp.concatenate([first[31:32], first[0:31]], axis=0)
            last = jnp.concatenate([last[1:32], last[0:1]], axis=0)
            o_ref[x, y] = (first + mid + last + b_ref[...]).astype(BF)


def _stage_kernel(w_hbm, w_ref, sems):
    copies = [
        pltpu.make_async_copy(w_hbm.at[pl.ds(9 * n, 9)], w_ref.at[pl.ds(9 * n, 9)], sems.at[n])
        for n in range(3)
    ]
    for copy in copies:
        copy.start()
    for copy in copies:
        copy.wait()


def _stage(w):
    return pl.pallas_call(
        _stage_kernel,
        out_shape=jax.ShapeDtypeStruct((27, COUT, D), BF),
        in_specs=[ANY],
        out_specs=VMEM,
        scratch_shapes=[pltpu.SemaphoreType.DMA((3,))],
        compiler_params=_params(42),
        cost_estimate=_cost(0, 21e6),
        name="stage_weights",
    )(w)


def _conv_inner(body, w):
    return pl.pallas_call(
        _conv_inner_kernel,
        out_shape=jax.ShapeDtypeStruct((3 * COUT, T), F32),
        in_specs=[VMEM, VMEM],
        out_specs=VMEM,
        compiler_params=_params(24),
        cost_estimate=_cost(2 * T * D * COUT * 18, 12e6),
        name="convolution_inner",
    )(body, w)


def _conv_outer(outer, edge, w, acc, bias):
    return pl.pallas_call(
        _conv_outer_kernel,
        out_shape=jax.ShapeDtypeStruct((2, 2, 32, COUT), BF),
        in_specs=[VMEM] * 5,
        out_specs=VMEM,
        compiler_params=_params(24),
        cost_estimate=_cost(2 * T * D * COUT * 9, 6e6),
        name="convolution_outer",
    )(outer, edge, w, acc, bias.reshape(1, COUT))


def _linear(y, xh, c, z, xl):
    return (y * 4 + xh * 2 + c) * 16 + z * 2 + xl


PLANES = [
    [_linear(y, xh, c, z, xl) for y in range(4) for xh in range(2) for xl in range(2)]
    for z in range(8)
    for c in range(2)
]


def _plane_swap(x):
    return lax.all_to_all(x, ("gx", "gy"), split_axis=0, concat_axis=0, tiled=True, axis_index_groups=PLANES)


def _core_swap(x):
    return lax.ppermute(x, "gx", [(i, i ^ 1) for i in range(16)])


def _along_z(x, d):
    return lax.ppermute(x, "gy", [(z * 2 + l, ((z + d) % 8) * 2 + l) for z in range(8) for l in range(2)])


def _across_z(x):
    return lax.ppermute(x, "gy", [(i, (i + 1 if i % 2 else i - 1) % 16) for i in range(16)])


def shards(tokens, w_qkv, w_out, norm_gain, norm_shift, w_conv, conv_bias):
    packed = _qkv(tokens.reshape(T, D), w_qkv)
    w_taps = jnp.transpose(w_conv, (0, 1, 2, 4, 3)).reshape(27, COUT // 16, D)
    packed, w_taps = lax.optimization_barrier((packed, w_taps))
    mine = _plane_swap(packed)
    taps = lax.all_gather(w_taps, "gx", axis=1, tiled=True)
    q_own, kv = mine[:, :HD], mine[:, HD:]
    up, down = _along_z(kv, 1), _along_z(kv, -1)
    q_sib = _core_swap(q_own)
    qa, m, acc = _first(q_own, q_sib, kv)
    chunks = [kv, up, down]
    for _ in range(2):
        later = (_along_z(up, 1), _along_z(down, -1))
        acc = _next(qa, acc, up, down)
        up, down = later
        chunks += [up, down]
    half = SRC // 2
    far = (_along_z(up[:half], 1), _along_z(down[half:], -1))
    acc = _next(qa, acc, up, down)
    acc = _last(qa, m, acc, far[0], far[1], chunks)
    att = _merge(acc, _core_swap(acc))
    back = _plane_swap(att).reshape(D, 3 * T)
    body, edge = _norm(back, w_out, norm_gain, norm_shift)
    body, edge, taps = lax.optimization_barrier((body, edge, taps))
    taps = _stage(taps)
    outer = _across_z(edge)
    inner = _conv_inner(body, taps)
    return _conv_outer(outer, edge, taps, inner, conv_bias)


def solution(mesh):
    return jax.shard_map(
        shards,
        mesh=mesh,
        in_specs=(
            P("gx", "gy", None, None),
            P(),
            P(),
            P(),
            P(),
            P(None, None, None, None, "gx"),
            P(),
        ),
        out_specs=P("gx", "gy", None, None),
        check_vma=False,
    )
```

```python
import functools
import math

import jax
import jax.numpy as jnp
from jax import lax
from jax.experimental import pallas as pl
from jax.experimental.pallas import tpu as pltpu
from jax.sharding import PartitionSpec as P

HEADS = 16
HD = 48
D = 768
COUT = 256
SRC = 16
T = 128
NQ = SRC * T
CK = SRC * T
Q2 = 2 * NQ
QT = 1024
QKV_CUTS = 3
QB, NT, KT = 2048, 512, 256
KROWS = 128
ORS = 64
SHIFT_ROW = 2 * HD
SUM_ROW = HD
M_ROW = 49
SENT = 56
SCALE = math.log2(math.e) / math.sqrt(HD)
SAFE_SUM = 2.0**100
VMEM = pl.BlockSpec(memory_space=pltpu.VMEM)
ANY = pl.BlockSpec(memory_space=pl.ANY)
BF = jnp.bfloat16
F32 = jnp.float32


def _params(mb=32):
    return pltpu.CompilerParams(vmem_limit_bytes=mb * 2**20)


def _cost(flops, nbytes, trans=0):
    return pl.CostEstimate(flops=int(flops), bytes_accessed=int(nbytes), transcendentals=int(trans))


def _qkv_kernel(x_hbm, w_hbm, o_ref, x_ref, w_ref, acc_ref, sems):
    copies = [pltpu.make_async_copy(x_hbm, x_ref, sems.at[0])]
    rows = D // QKV_CUTS
    for n in range(QKV_CUTS):
        part = pl.ds(n * rows, rows)
        copies.append(pltpu.make_async_copy(w_hbm.at[part], w_ref.at[part], sems.at[n + 1]))
    for copy in copies:
        copy.start()
    copies[0].wait()
    for n in range(QKV_CUTS):
        copies[n + 1].wait()
        part = slice(n * rows, (n + 1) * rows)
        y = jnp.dot(x_ref[:, part], w_ref[part, :], preferred_element_type=F32)
        acc_ref[...] = y if n == 0 else acc_ref[...] + y
    for part in range(3):
        yt = acc_ref[:, part * D : (part + 1) * D].T.astype(BF)
        for h in range(HEADS):
            o_ref[h, part * HD : (part + 1) * HD, :] = yt[h * HD : (h + 1) * HD, :]


def _qkv(x, w):
    return pl.pallas_call(
        _qkv_kernel,
        out_shape=jax.ShapeDtypeStruct((HEADS, 3 * HD, T), BF),
        in_specs=[ANY, ANY],
        out_specs=VMEM,
        scratch_shapes=[
            pltpu.VMEM((T, D), BF),
            pltpu.VMEM((D, 3 * D), BF),
            pltpu.VMEM((T, 3 * D), F32),
            pltpu.SemaphoreType.DMA((QKV_CUTS + 1,)),
        ],
        compiler_params=_params(58),
        cost_estimate=_cost(2 * T * D * 3 * D, 5e6),
        name="qkv_projection",
    )(x, w)


def _fill_chunk(kv_ref, kp_ref, vp_ref, base):
    row = lax.broadcasted_iota(jnp.int32, (KROWS - 2 * HD, T), 0)
    shift_on = jnp.where(row < 3, 1.0, 0.0).astype(BF)
    vrow = lax.broadcasted_iota(jnp.int32, (ORS - HD, T), 0)
    ones = jnp.where(vrow == 0, 1.0, 0.0).astype(BF)
    for s in range(SRC):
        kt = kv_ref[s, 0:HD, :]
        block = jnp.concatenate([kt, kt, shift_on], axis=0)
        at = base + s * T
        kp_ref[at : at + T, :] = block.T
        vp_ref[0:HD, at : at + T] = kv_ref[s, HD : 2 * HD, :]
        vp_ref[HD:ORS, at : at + T] = ones


def _set_shift(qa_ref, cols, m):
    hi = m.astype(BF)
    rest = m - hi.astype(F32)
    mid = rest.astype(BF)
    low = (rest - mid.astype(F32)).astype(BF)
    row = lax.broadcasted_iota(jnp.int32, (16, m.shape[1]), 0)
    rows = jnp.where(
        row == 0, hi.astype(F32), jnp.where(row == 1, mid.astype(F32), jnp.where(row == 2, low.astype(F32), 0.0))
    )
    qa_ref[SHIFT_ROW : SHIFT_ROW + 16, cols] = (-rows).astype(BF)


def _tile(i):
    return pl.ds(pl.multiple_of(i * QT, QT), QT)


def _accumulate(qa_ref, kp_ref, vp_ref, acc_in, acc_out, chunks):
    keys, tiles = chunks * CK // KT, QB // NT

    def body(i, carry):
        def cols(t):
            return pl.ds(pl.multiple_of(i * QB + t * NT, NT), NT)

        q = [qa_ref[:, cols(t)] for t in range(tiles)]
        acc = [acc_in[:, cols(t)] if acc_in is not None else jnp.zeros((ORS, NT), F32) for t in range(tiles)]
        steps = [(k, t) for k in range(keys) for t in range(tiles)]
        scores, weights = {}, {}
        for n in range(len(steps) + 2):
            if n < len(steps):
                k, t = steps[n]
                scores[n] = jnp.dot(kp_ref[k * KT : (k + 1) * KT, :], q[t], preferred_element_type=F32)
            if 0 <= n - 1 < len(steps):
                weights[n - 1] = jnp.exp2(scores.pop(n - 1)).astype(BF)
            if 0 <= n - 2:
                k, t = steps[n - 2]
                acc[t] = acc[t] + jnp.dot(
                    vp_ref[:, k * KT : (k + 1) * KT], weights.pop(n - 2), preferred_element_type=F32
                )
        for t in range(tiles):
            acc_out[:, cols(t)] = acc[t]
        return carry

    lax.fori_loop(0, Q2 // QB, body, 0)


def _first_kernel(q_own, q_sib, kv_ref, qa_ref, m_ref, acc_ref, kp_ref, vp_ref):
    _fill_chunk(kv_ref, kp_ref, vp_ref, 0)
    for part, q_ref in enumerate((q_own, q_sib)):
        for s in range(SRC):
            cols = pl.ds(part * NQ + s * T, T)
            q = q_ref[s, 0:HD, :].astype(F32) * SCALE
            hi = q.astype(BF)
            qa_ref[0:HD, cols] = hi
            qa_ref[HD : 2 * HD, cols] = (q - hi.astype(F32)).astype(BF)
    qa_ref[SHIFT_ROW:KROWS, :] = jnp.zeros((KROWS - SHIFT_ROW, Q2), BF)

    def start(i, carry):
        cols = _tile(i)
        s = jnp.dot(kp_ref[0:256, :], qa_ref[:, cols], preferred_element_type=F32)
        m = jnp.max(s, axis=0, keepdims=True)
        m_ref[:, cols] = jnp.broadcast_to(m, (8, QT))
        _set_shift(qa_ref, cols, m)
        return carry

    lax.fori_loop(0, Q2 // QT, start, 0)
    _accumulate(qa_ref, kp_ref, vp_ref, None, acc_ref, 1)


def _next_kernel(chunks, qa_ref, acc_in, *refs):
    kvs, (acc_out, kp_ref, vp_ref) = refs[:chunks], refs[chunks:]
    for c in range(chunks):
        _fill_chunk(kvs[c], kp_ref, vp_ref, c * CK)
    _accumulate(qa_ref, kp_ref, vp_ref, acc_in, acc_out, chunks)


def _redo(qa_ref, m_ref, acc_ref, kp_ref, vp_ref, kvs, kv_a, kv_b, buf, sem):
    def load(c):
        for n, ref in enumerate(kvs):

            @pl.when(c == n)
            def _():
                copy = pltpu.make_async_copy(ref, buf, sem)
                copy.start()
                copy.wait()

        @pl.when(c == len(kvs))
        def _():
            buf[0 : SRC // 2] = kv_a[...]
            buf[SRC // 2 : SRC] = kv_b[...]

        _fill_chunk(buf, kp_ref, vp_ref, 0)

    qa_ref[SHIFT_ROW:KROWS, :] = jnp.zeros((KROWS - SHIFT_ROW, Q2), BF)

    def find(c, carry):
        load(c)

        def body(i, inner):
            cols = _tile(i)
            s = jnp.dot(kp_ref[0:CK, :], qa_ref[:, cols], preferred_element_type=F32)
            m_ref[:, cols] = jnp.maximum(m_ref[:, cols], jnp.max(s, axis=0, keepdims=True))
            return inner

        return lax.fori_loop(0, Q2 // QT, body, carry)

    lax.fori_loop(0, len(kvs) + 1, find, 0)

    def shift(i, carry):
        cols = _tile(i)
        _set_shift(qa_ref, cols, m_ref[0:1, cols])
        acc_ref[:, cols] = jnp.zeros((ORS, QT), F32)
        return carry

    lax.fori_loop(0, Q2 // QT, shift, 0)

    def add(c, carry):
        load(c)
        _accumulate(qa_ref, kp_ref, vp_ref, acc_ref, acc_ref, 1)
        return carry

    lax.fori_loop(0, len(kvs) + 1, add, 0)


def _last_kernel(qa_in, m_in, acc_in, kv_a, kv_b, *refs):
    kvs, (sent_ref, out_ref, qa_ref, m_ref, kp_ref, vp_ref, buf, sem) = refs[:7], refs[7:]
    half = SRC // 2
    for s in range(half):
        buf[s, :, :] = kv_a[s, :, :]
        buf[half + s, :, :] = kv_b[s, :, :]
    _fill_chunk(buf, kp_ref, vp_ref, 0)
    _accumulate(qa_in, kp_ref, vp_ref, acc_in, out_ref, 1)
    m_ref[...] = m_in[...]
    good = jnp.max(out_ref[SUM_ROW : SUM_ROW + 1, :]) < SAFE_SUM

    @pl.when(jnp.logical_not(good))
    def _():
        qa_ref[...] = qa_in[...]
        _redo(qa_ref, m_ref, out_ref, kp_ref, vp_ref, kvs, kv_a, kv_b, buf, sem)

    sent_ref[0:HD, :] = out_ref[0:HD, :]
    row = lax.broadcasted_iota(jnp.int32, (8, Q2), 0)
    sent_ref[HD:SENT, :] = jnp.where(row == 0, out_ref[HD:SENT, :], m_ref[...])


def _pair_cost(chunks):
    return _cost(2 * Q2 * CK * 512 * chunks, 4e6, Q2 * CK * chunks)


def _scratch(chunks):
    return [pltpu.VMEM((chunks * CK, KROWS), BF), pltpu.VMEM((ORS, chunks * CK), BF)]


def _first(q_own, q_sib, kv):
    return pl.pallas_call(
        _first_kernel,
        out_shape=(
            jax.ShapeDtypeStruct((KROWS, Q2), BF),
            jax.ShapeDtypeStruct((8, Q2), F32),
            jax.ShapeDtypeStruct((ORS, Q2), F32),
        ),
        in_specs=[VMEM] * 3,
        out_specs=(VMEM,) * 3,
        scratch_shapes=_scratch(1),
        compiler_params=_params(),
        cost_estimate=_pair_cost(1),
        name="attend_own",
    )(q_own, q_sib, kv)


def _next(qa, acc, *kvs):
    n = len(kvs)
    return pl.pallas_call(
        functools.partial(_next_kernel, n),
        out_shape=jax.ShapeDtypeStruct((ORS, Q2), F32),
        in_specs=[VMEM] * (2 + n),
        out_specs=VMEM,
        scratch_shapes=_scratch(n),
        compiler_params=_params(),
        cost_estimate=_pair_cost(n),
        name="attend_ring",
    )(qa, acc, *kvs)


def _last(qa, m, acc, kv_a, kv_b, kvs):
    return pl.pallas_call(
        _last_kernel,
        out_shape=jax.ShapeDtypeStruct((SENT, Q2), F32),
        in_specs=[VMEM] * 5 + [ANY] * 7,
        out_specs=VMEM,
        scratch_shapes=[
            pltpu.VMEM((ORS, Q2), F32),
            pltpu.VMEM((KROWS, Q2), BF),
            pltpu.VMEM((8, Q2), F32),
            *_scratch(1),
            pltpu.VMEM((SRC, 2 * HD, T), BF),
            pltpu.SemaphoreType.DMA,
        ],
        compiler_params=_params(),
        cost_estimate=_pair_cost(1),
        name="attend_last",
    )(qa, m, acc, kv_a, kv_b, *kvs)


def _merge_kernel(a_ref, b_ref, o_ref, own_ref, sib_ref):
    c = lax.rem(lax.axis_index("gx"), 2)
    for dst, mine, other in ((own_ref, 0, NQ), (sib_ref, NQ, 0)):
        a, b = slice(mine, mine + NQ), slice(other, other + NQ)
        ma, mb = a_ref[M_ROW : M_ROW + 1, a], b_ref[M_ROW : M_ROW + 1, b]
        top = jnp.maximum(ma, mb)
        wa, wb = jnp.exp2(ma - top), jnp.exp2(mb - top)
        total = a_ref[SUM_ROW : SUM_ROW + 1, a] * wa + b_ref[SUM_ROW : SUM_ROW + 1, b] * wb
        out = (a_ref[0:HD, a] * wa + b_ref[0:HD, b] * wb) / total
        for s in range(SRC):
            dst[s, :, :] = out[:, s * T : (s + 1) * T]
    lane = lax.broadcasted_iota(jnp.int32, (HD, T), 1)
    first = lane < 64
    y = lax.rem(lax.div(lane, 32), 2)
    for k in range(8):
        after, before = lax.rem(k + c, 8), lax.rem(k + 7 + c, 8)
        for xl in range(2):
            s = k * 2 + xl
            o_ref[s, :, 0:T] = own_ref[s].astype(BF)
            sides = jnp.where(first, sib_ref[after * 2 + xl], sib_ref[before * 2 + xl])
            o_ref[s, :, T : 2 * T] = sides.astype(BF)
            corners = jnp.where(first, sib_ref[after * 2 + 1 - xl], sib_ref[before * 2 + 1 - xl])
            corners = pltpu.roll(corners, 32 if xl == 0 else T - 32, 1)
            o_ref[s, :, 2 * T : 3 * T] = jnp.where(y == xl, own_ref[k * 2 + 1 - xl], corners).astype(BF)


def _merge(a, b):
    return pl.pallas_call(
        _merge_kernel,
        out_shape=jax.ShapeDtypeStruct((SRC, HD, 3 * T), BF),
        in_specs=[VMEM, VMEM],
        out_specs=VMEM,
        scratch_shapes=[pltpu.VMEM((SRC, HD, T), F32)] * 2,
        compiler_params=_params(16),
        cost_estimate=_cost(1e6, 3e6),
        name="merge_cores",
    )(a, b)


def _norm_kernel(att_ref, w_ref, gain_ref, shift_ref, body_ref, edge_ref):
    xl = lax.rem(lax.axis_index("gy"), 2)
    for part in range(3):
        att = att_ref[:, part * T : (part + 1) * T].astype(F32).T.astype(BF)
        v = jnp.dot(att, w_ref[...], preferred_element_type=F32)
        center = jnp.mean(v, axis=-1, keepdims=True)
        spread = jnp.mean((v - center) ** 2, axis=-1, keepdims=True)
        n = ((v - center) / jnp.sqrt(spread + 1e-05) * gain_ref[...] + shift_ref[...]).astype(BF)
        for x in range(2):
            for y in range(2):
                rows = n[(x * 2 + y) * 32 : (x * 2 + y + 1) * 32]
                side = 3 - 3 * x
                layer = y + xl * (1 - 2 * y)
                if part == 0:
                    body_ref[layer, 1 + x] = rows
                elif part == 1:
                    body_ref[layer, side] = rows
                else:
                    inner = xl if y == 1 else 1 - xl
                    body_ref[2, inner * (1 + x) + (1 - inner) * side] = rows
    edge_ref[...] = body_ref[0]


def _norm(att, w, gain, shift):
    return pl.pallas_call(
        _norm_kernel,
        out_shape=(jax.ShapeDtypeStruct((3, 4, 32, D), BF), jax.ShapeDtypeStruct((4, 32, D), BF)),
        in_specs=[VMEM] * 4,
        out_specs=(VMEM, VMEM),
        compiler_params=_params(16),
        cost_estimate=_cost(6 * T * D * D, 3e6),
        name="project_norm",
    )(att, w, gain.reshape(1, D), shift.reshape(1, D))


def _taps(w_ref, a, layer, xl):
    b = layer + xl * (2 - 2 * layer)
    return w_ref[pl.ds((a * 3 + b) * 3, 3)].reshape(3 * COUT, D)


def _product(w, window):
    return lax.dot_general(
        w, window.reshape(T, D), (((1,), (1,)), ((), ())), preferred_element_type=F32
    )


def _conv_inner_kernel(body_ref, w_ref, acc_ref):
    xl = lax.rem(lax.axis_index("gy"), 2)
    total = None
    for a in range(3):
        for layer in (1, 2):
            y = _product(_taps(w_ref, a, layer, xl), body_ref[layer - 1 : layer + 1, a : a + 2])
            total = y if total is None else total + y
    acc_ref[...] = total


def _conv_outer_kernel(outer_ref, edge_ref, w_ref, acc_ref, b_ref, o_ref):
    xl = lax.rem(lax.axis_index("gy"), 2)
    total = acc_ref[...]
    for a in range(3):
        window = jnp.concatenate([outer_ref[a : a + 2], edge_ref[a : a + 2]], axis=0)
        total = total + _product(_taps(w_ref, a, 0, xl), window)
    total = total.T
    for layer in range(2):
        y = layer + xl * (1 - 2 * layer)
        for x in range(2):
            at = (layer * 2 + x) * 32
            rows = slice(at, at + 32)
            first = total[rows, 0:COUT]
            mid = total[rows, COUT : 2 * COUT]
            last = total[rows, 2 * COUT : 3 * COUT]
            first = jnp.concatenate([first[31:32], first[0:31]], axis=0)
            last = jnp.concatenate([last[1:32], last[0:1]], axis=0)
            o_ref[x * 2 + y] = (first + mid + last + b_ref[...]).astype(BF)


def _stage_kernel(w_hbm, w_ref, sems):
    copies = [
        pltpu.make_async_copy(w_hbm.at[pl.ds(9 * n, 9)], w_ref.at[pl.ds(9 * n, 9)], sems.at[n])
        for n in range(3)
    ]
    for copy in copies:
        copy.start()
    for copy in copies:
        copy.wait()


def _stage(w):
    return pl.pallas_call(
        _stage_kernel,
        out_shape=jax.ShapeDtypeStruct((27, COUT, D), BF),
        in_specs=[ANY],
        out_specs=VMEM,
        scratch_shapes=[pltpu.SemaphoreType.DMA((3,))],
        compiler_params=_params(42),
        cost_estimate=_cost(0, 21e6),
        name="stage_weights",
    )(w)


def _conv_inner(body, w):
    return pl.pallas_call(
        _conv_inner_kernel,
        out_shape=jax.ShapeDtypeStruct((3 * COUT, T), F32),
        in_specs=[VMEM, VMEM],
        out_specs=VMEM,
        compiler_params=_params(24),
        cost_estimate=_cost(2 * T * D * COUT * 18, 12e6),
        name="convolution_inner",
    )(body, w)


def _conv_outer(outer, edge, w, acc, bias):
    return pl.pallas_call(
        _conv_outer_kernel,
        out_shape=jax.ShapeDtypeStruct((4, 32, COUT), BF),
        in_specs=[VMEM] * 5,
        out_specs=VMEM,
        compiler_params=_params(24),
        cost_estimate=_cost(2 * T * D * COUT * 9, 6e6),
        name="convolution_outer",
    )(outer, edge, w, acc, bias.reshape(1, COUT))


def _linear(y, xh, c, z, xl):
    return (y * 4 + xh * 2 + c) * 16 + z * 2 + xl


PLANES = [
    [_linear(y, xh, c, z, xl) for y in range(4) for xh in range(2) for xl in range(2)]
    for z in range(8)
    for c in range(2)
]


def _plane_swap(x):
    return lax.all_to_all(x, ("gx", "gy"), split_axis=0, concat_axis=0, tiled=True, axis_index_groups=PLANES)


def _core_swap(x):
    return lax.ppermute(x, "gx", [(i, i ^ 1) for i in range(16)])


def _along_z(x, d):
    return lax.ppermute(x, "gy", [(z * 2 + l, ((z + d) % 8) * 2 + l) for z in range(8) for l in range(2)])


def _across_z(x):
    return lax.ppermute(x, "gy", [(i, (i + 1 if i % 2 else i - 1) % 16) for i in range(16)])


def shards(tokens, w_qkv, w_out, norm_gain, norm_shift, w_conv, conv_bias):
    packed = _qkv(tokens.reshape(T, D), w_qkv)
    w_taps = jnp.transpose(w_conv, (0, 1, 2, 4, 3)).reshape(27, COUT // 16, D)
    packed, w_taps = lax.optimization_barrier((packed, w_taps))
    mine = _plane_swap(packed)
    taps = lax.all_gather(w_taps, "gx", axis=1, tiled=True)
    q_own, kv = mine[:, :HD], mine[:, HD:]
    up, down = _along_z(kv, 1), _along_z(kv, -1)
    q_sib = _core_swap(q_own)
    qa, m, acc = _first(q_own, q_sib, kv)
    chunks = [kv, up, down]
    for _ in range(2):
        later = (_along_z(up, 1), _along_z(down, -1))
        acc = _next(qa, acc, up, down)
        up, down = later
        chunks += [up, down]
    half = SRC // 2
    far = (_along_z(up[:half], 1), _along_z(down[half:], -1))
    acc = _next(qa, acc, up, down)
    acc = _last(qa, m, acc, far[0], far[1], chunks)
    att = _merge(acc, _core_swap(acc))
    back = _plane_swap(att).reshape(D, 3 * T)
    body, edge = _norm(back, w_out, norm_gain, norm_shift)
    body, edge, taps = lax.optimization_barrier((body, edge, taps))
    taps = _stage(taps)
    outer = _across_z(edge)
    inner = _conv_inner(body, taps)
    return _conv_outer(outer, edge, taps, inner, conv_bias).reshape(2, 2, 32, COUT)


def solution(mesh):
    return jax.shard_map(
        shards,
        mesh=mesh,
        in_specs=(
            P("gx", "gy", None, None),
            P(),
            P(),
            P(),
            P(),
            P(None, None, None, None, "gx"),
            P(),
        ),
        out_specs=P("gx", "gy", None, None),
        check_vma=False,
    )
```
